32 devices in a mesh: row: 4 (over z), col: 8 (over y, x, core).
Axes of the slice: x: 2, y: 2, z: 4, core: 2. Of those that a mesh axis runs over, the one named last changes fastest.
Arguments:
- tokens: bfloat16 [96, 12288], P('col', 'row'), may hold values from -6 to 6
- up_weight: bfloat16 [12288, 49152], P('row', 'col'), may hold values from -0.0546875 to 0.0546875
- up_bias: float32 [49152], P('col'), may hold values from -3 to 3
- down_weight: bfloat16 [49152, 12288], P('col', 'row'), may hold values from -0.02734375 to 0.02734375
- down_bias: float32 [12288], P('row'), may hold values from -3 to 3
Outputs:
- layer_out: bfloat16 [96, 12288], P('col', 'row')
The draws below stay inside these ranges and needn't reach their ends.
All inputs are finite; a program needn't handle non-finite values.
Results may differ from the reference program's by a relative error of at most 0.0034.
Values may be sent and summed in bfloat16 or wider, within the bound.
A program may use at most 128 MiB of HBM per device.

```python
import jax
import jax.numpy as jnp

D = 12288
FF = 49152
TOKENS = 96


def levels(key, shape, shards, smallest, largest):
    gain = 1.0
    for axis_at, blocks in shards:
        steps = jax.random.uniform(jax.random.fold_in(jax.random.fold_in(key, 6), axis_at), (blocks,), jnp.float32, smallest / len(shards), largest / len(shards))
        gain = gain * jnp.repeat(jnp.exp(steps), shape[axis_at] // blocks).reshape((-1,) + (1,) * (len(shape) - 1 - axis_at))
    return gain


def noise(own_key, dims, deviation, reach, shards=(), held_as=jnp.bfloat16):
    result = jax.random.normal(own_key, dims, jnp.float32) * deviation
    if len(shards) > 0:
        result = levels(own_key, dims, shards, -0.22, 0.18) * result
    return jnp.clip(result, min=-reach, max=reach).astype(held_as)


def setup_inputs(seed: int = 0) -> dict:
    key_list = jax.random.split(jax.random.key(seed), 6)
    tokens = noise(key_list[0], (TOKENS, D), 1.0, 6.0, ((0, 8), (1, 4)))
    up_weight = noise(key_list[1], (D, FF), D ** -0.5, 0.0546875, ((0, 4), (1, 8)))
    up_bias = noise(key_list[2], (FF,), 0.5, 3.0, ((0, 8),), jnp.float32)
    down_weight = noise(key_list[3], (FF, D), FF ** -0.5, 0.02734375, ((0, 8), (1, 4)))
    down_bias = noise(key_list[4], (D,), 0.5, 3.0, ((0, 4),), jnp.float32)
    return dict(tokens=tokens, up_weight=up_weight, up_bias=up_bias, down_weight=down_weight, down_bias=down_bias)


def reference(tokens, up_weight, up_bias, down_weight, down_bias):
    pre_act = jnp.dot(tokens, up_weight, preferred_element_type=jnp.float32) + up_bias
    activated = jax.nn.gelu(pre_act, approximate=True).astype(jnp.bfloat16)
    branch = jnp.dot(activated, down_weight, preferred_element_type=jnp.float32)
    return (tokens.astype(jnp.float32) + branch + down_bias).astype(jnp.bfloat16)
```

```python
import functools

import jax
import jax.numpy as jnp
from jax import lax
from jax.experimental import pallas as pl
from jax.experimental.pallas import tpu as pltpu
from jax.sharding import PartitionSpec as P

CHUNK = 256
SPLIT = 4
MESH = pl.DeviceIdType.MESH


def gelu(v):
    return 0.5 * v * (1.0 + jnp.tanh(0.7978845608028654 * (v + 0.044715 * (v * v * v))))


def kernel(
    rows, cols, tok_ref, up_ref, ub_ref, down_ref, db_ref, out_ref,
    ubuf, dbuf, gath, xg, part, sbuf, rin, rc, act, acc, packf, own, sib_out, sib_in, peer_out, peer_in,
    usem, dsem, g_send, g_recv, f_send, in_send, in_recv, out_send, c_recv,
    s1_send, s1_recv, s2_send, s2_recv,
):
    tok, feat = tok_ref.shape
    wide = feat // SPLIT
    n = up_ref.shape[1] // CHUNK
    u_slots, d_slots = ubuf.shape[0], dbuf.shape[0]
    chips = cols // 2
    half = rows // 2
    r, c = lax.axis_index("row"), lax.axis_index("col")
    chip, core = c // 2, lax.rem(c, 2)
    sib = chip * 2 + 1 - core
    low = r < half
    depth = jnp.where(low, half - 1 - r, r - half)
    inner = jnp.where(low, r + 1, r - 1)
    outer = jnp.where(low, r - 1, r + 1)
    centre, end = depth == 0, depth == half - 1

    def peer(k):
        return lax.rem(chip + k, chips)

    def load_up(j):
        at = pl.ds(pl.multiple_of(j * CHUNK, CHUNK), CHUNK)
        slot = lax.rem(j, u_slots)
        return pltpu.make_async_copy(up_ref.at[:, at], ubuf.at[slot], usem.at[slot])

    def load_down(j):
        at = pl.ds(pl.multiple_of(j * CHUNK, CHUNK), CHUNK)
        slot = lax.rem(j, d_slots)
        return pltpu.make_async_copy(down_ref.at[at, :], dbuf.at[slot], dsem.at[slot])

    def each(lo, hi, body):
        def step(i, carry):
            body(i)
            return carry
        lax.fori_loop(lo, hi, step, 0)

    each(0, u_slots, lambda j: load_up(j).start())

    barrier = pltpu.get_barrier_semaphore()

    def greet(row, col):
        pl.semaphore_signal(barrier, inc=1, device_id=(row, col), device_id_type=MESH)

    greet(r, sib)
    each(1, chips, lambda k: greet(r, peer(k) * 2 + core))
    greet(inner, c)

    @pl.when(jnp.logical_not(end))
    def _():
        greet(outer, c)

    mine = tok_ref[...].astype(jnp.float32)
    own[...] = jnp.zeros_like(own)
    for q in range(SPLIT):
        own[q * tok:(q + 1) * tok, :] = mine[:, q * wide:(q + 1) * wide]
    gath[c] = own[...].astype(jnp.bfloat16)

    @pl.when(end)
    def _():
        pl.semaphore_wait(barrier, chips + 1)

    @pl.when(jnp.logical_not(end))
    def _():
        pl.semaphore_wait(barrier, chips + 2)

    def gather_copy(src, send, col):
        return pltpu.make_async_remote_copy(
            src_ref=gath.at[src], dst_ref=gath.at[src], send_sem=send, recv_sem=g_recv.at[src],
            device_id=(r, col), device_id_type=MESH)

    each(1, chips, lambda k: gather_copy(c, g_send.at[k], peer(k) * 2 + core).start())
    gather_copy(c, g_send.at[0], sib).start()

    def forward(k):
        src = peer(k) * 2 + core
        gather_copy(src, f_send.at[k], sib).wait_recv()
        gather_copy(src, f_send.at[k], sib).start()

    each(1, chips, forward)
    each(0, d_slots, lambda j: load_down(j).start())
    each(0, chips, lambda k: gather_copy(peer(k) * 2 + 1 - core, g_send.at[0], sib).wait_recv())
    each(1, chips, lambda k: gather_copy(c, g_send.at[k], sib).wait_send())
    gather_copy(c, g_send.at[0], sib).wait_send()
    each(1, chips, lambda k: gather_copy(peer(k) * 2 + core, f_send.at[k], sib).wait_send())

    for d in range(cols):
        slab = gath[d].astype(jnp.float32)
        for q in range(SPLIT):
            acc[d * tok:(d + 1) * tok, q * wide:(q + 1) * wide] = slab[q * tok:(q + 1) * tok, :]
    xg[...] = acc[...].astype(jnp.bfloat16)
    acc[...] = jnp.zeros_like(acc)

    def inward(j, dst, sem):
        return pltpu.make_async_remote_copy(
            src_ref=sbuf.at[j], dst_ref=dst.at[j], send_sem=in_send.at[j], recv_sem=sem.at[j],
            device_id=(inner, c), device_id_type=MESH)

    def outward(j):
        return pltpu.make_async_remote_copy(
            src_ref=act.at[j], dst_ref=rc.at[j], send_sem=out_send.at[j], recv_sem=c_recv.at[j],
            device_id=(outer, c), device_id_type=MESH)

    lag_in = 2 * (half - 1 - depth)
    lag_out = 2 * (half - 1) + 3 + 3 * depth
    ticks = n + 2 * (half - 1) + 3 + 3 * (half - 1)

    def tick(t):
        @pl.when(t < n)
        def _():
            load_up(t).wait()
            part[t] = jnp.dot(xg[...], ubuf[lax.rem(t, u_slots)], preferred_element_type=jnp.float32)

            @pl.when(t + u_slots < n)
            def _():
                load_up(t + u_slots).start()

        a = t - lag_in

        @pl.when((a >= 0) & (a < n))
        def _():
            @pl.when(jnp.logical_not(end))
            def _():
                inward(a, rin, in_recv).wait_recv()
                part[a] = part[a] + rin[a].astype(jnp.float32)

            sbuf[a] = part[a].astype(jnp.bfloat16)

            @pl.when(centre)
            def _():
                inward(a, rc, c_recv).start()

            @pl.when(jnp.logical_not(centre))
            def _():
                inward(a, rin, in_recv).start()

        b = t - lag_out

        @pl.when((b >= 0) & (b < n))
        def _():
            outward(b).wait_recv()

            @pl.when(centre)
            def _():
                bias = ub_ref[:, pl.ds(pl.multiple_of(b * CHUNK, CHUNK), CHUNK)]
                act[b] = gelu(part[b] + rc[b].astype(jnp.float32) + bias).astype(jnp.bfloat16)

            @pl.when(jnp.logical_not(centre))
            def _():
                act[b] = rc[b]

            @pl.when(jnp.logical_not(end))
            def _():
                outward(b).start()

            load_down(b).wait()
            acc[...] += jnp.dot(act[b], dbuf[lax.rem(b, d_slots)], preferred_element_type=jnp.float32)

            @pl.when(b + d_slots < n)
            def _():
                load_down(b + d_slots).start()

    each(0, ticks, tick)

    packf[...] = jnp.zeros_like(packf)
    for d in range(cols):
        for q in range(SPLIT):
            packf[d, q * tok:(q + 1) * tok, :] = acc[d * tok:(d + 1) * tok, q * wide:(q + 1) * wide]

    def to_sibling(k):
        return pltpu.make_async_remote_copy(
            src_ref=sib_out.at[k], dst_ref=sib_in.at[k], send_sem=s1_send.at[k], recv_sem=s1_recv.at[k],
            device_id=(r, sib), device_id_type=MESH)

    def to_peer(k):
        return pltpu.make_async_remote_copy(
            src_ref=peer_out.at[k], dst_ref=peer_in.at[k], send_sem=s2_send.at[k], recv_sem=s2_recv.at[k],
            device_id=(r, peer(k) * 2 + core), device_id_type=MESH)

    def first(i):
        k = lax.rem(i, chips)
        sib_out[k] = packf[peer(k) * 2 + 1 - core].astype(jnp.bfloat16)
        to_sibling(k).start()

    def second(k):
        to_sibling(k).wait_recv()
        peer_out[k] = (packf[peer(k) * 2 + core] + sib_in[k].astype(jnp.float32)).astype(jnp.bfloat16)
        to_peer(k).start()

    each(1, chips + 1, first)
    each(1, chips, second)
    to_sibling(0).wait_recv()
    own[...] = packf[c] + sib_in[0].astype(jnp.float32)

    def third(k):
        to_peer(k).wait_recv()
        own[...] += peer_in[k].astype(jnp.float32)

    each(1, chips, third)
    for q in range(SPLIT):
        at = slice(q * wide, (q + 1) * wide)
        out_ref[:, at] = (
            tok_ref[:, at].astype(jnp.float32) + own[q * tok:(q + 1) * tok, :] + db_ref[:, at]
        ).astype(out_ref.dtype)

    each(0, chips, lambda k: to_sibling(k).wait_send())
    each(1, chips, lambda k: to_peer(k).wait_send())
    each(0, n, lambda j: inward(j, rin, in_recv).wait_send())

    @pl.when(jnp.logical_not(end))
    def _():
        each(0, n, lambda j: outward(j).wait_send())


def on_device(rows, cols, tokens, up_weight, up_bias, down_weight, down_bias):
    tok, feat = tokens.shape
    hidden = up_weight.shape[1]
    n = hidden // CHUNK
    m = tok * cols
    chips = cols // 2
    chunk_bytes = feat * CHUNK * 2
    u_slots = max(1, min(n, 28 * 1024 * 1024 // chunk_bytes))
    d_slots = max(1, min(n, 18 * 1024 * 1024 // chunk_bytes))
    tall = -(-tok * SPLIT // 16) * 16
    wide = feat // SPLIT
    bf16, f32 = jnp.bfloat16, jnp.float32
    vmem, dma = pltpu.VMEM, pltpu.SemaphoreType.DMA
    in_vmem = pl.BlockSpec(memory_space=pltpu.VMEM)
    in_place = pl.BlockSpec(memory_space=pl.ANY)
    return pl.pallas_call(
        functools.partial(kernel, rows, cols),
        out_shape=jax.ShapeDtypeStruct((tok, feat), bf16),
        in_specs=[in_vmem, in_place, in_vmem, in_place, in_vmem],
        out_specs=in_vmem,
        scratch_shapes=[
            vmem((u_slots, feat, CHUNK), bf16),
            vmem((d_slots, CHUNK, feat), bf16),
            vmem((cols, tall, wide), bf16),
            vmem((m, feat), bf16),
            vmem((n, m, CHUNK), f32),
            vmem((n, m, CHUNK), bf16),
            vmem((n, m, CHUNK), bf16),
            vmem((n, m, CHUNK), bf16),
            vmem((n, m, CHUNK), bf16),
            vmem((m, feat), f32),
            vmem((cols, tall, wide), f32),
            vmem((tall, wide), f32),
            vmem((chips, tall, wide), bf16),
            vmem((chips, tall, wide), bf16),
            vmem((chips, tall, wide), bf16),
            vmem((chips, tall, wide), bf16),
            dma((u_slots,)),
            dma((d_slots,)),
            dma((chips,)),
            dma((cols,)),
            dma((chips,)),
            dma((n,)),
            dma((n,)),
            dma((n,)),
            dma((n,)),
            dma((chips,)),
            dma((chips,)),
            dma((chips,)),
            dma((chips,)),
        ],
        cost_estimate=pl.CostEstimate(
            flops=4 * m * feat * hidden, bytes_accessed=4 * feat * hidden, transcendentals=m * hidden),
        compiler_params=pltpu.CompilerParams(
            collective_id=0, has_side_effects=True, vmem_limit_bytes=63 * 1024 * 1024),
    )(tokens, up_weight, up_bias.reshape(1, -1), down_weight, down_bias.reshape(1, -1))


def solution(mesh):
    placed = (P("col", "row"), P("row", "col"), P("col"), P("col", "row"), P("row"))
    body = functools.partial(on_device, mesh.shape["row"], mesh.shape["col"])
    return jax.shard_map(body, mesh=mesh, in_specs=placed, out_specs=P("col", "row"), check_vma=False)
```

```python
import functools

import jax
import jax.numpy as jnp
from jax import lax
from jax.experimental import pallas as pl
from jax.experimental.pallas import tpu as pltpu
from jax.sharding import PartitionSpec as P

CHUNK = 256
SPLIT = 4
MESH = pl.DeviceIdType.MESH


def gelu(v):
    return 0.5 * v * (1.0 + jnp.tanh(0.7978845608028654 * (v + 0.044715 * (v * v * v))))


def kernel(
    rows, cols, tok_ref, up_ref, ub_ref, down_ref, db_ref, out_ref,
    ubuf, dbuf, gath, xg, part, sbuf, rin, rc, act, acc, packf, own, sib_out, sib_in, peer_out, peer_in,
    usem, dsem, g_send, g_recv, f_send, in_send, in_recv, out_send, c_recv,
    s1_send, s1_recv, s2_send, s2_recv,
):
    tok, feat = tok_ref.shape
    wide = feat // SPLIT
    n = up_ref.shape[1] // CHUNK
    u_slots, d_slots = ubuf.shape[0], dbuf.shape[0]
    chips = cols // 2
    half = rows // 2
    r, c = lax.axis_index("row"), lax.axis_index("col")
    chip, core = c // 2, lax.rem(c, 2)
    sib = chip * 2 + 1 - core
    low = r < half
    depth = jnp.where(low, half - 1 - r, r - half)
    inner = jnp.where(low, r + 1, r - 1)
    outer = jnp.where(low, r - 1, r + 1)
    centre, end = depth == 0, depth == half - 1

    def peer(k):
        return lax.rem(chip + k, chips)

    def load_up(j):
        at = pl.ds(pl.multiple_of(j * CHUNK, CHUNK), CHUNK)
        slot = lax.rem(j, u_slots)
        return pltpu.make_async_copy(up_ref.at[:, at], ubuf.at[slot], usem.at[slot])

    def load_down(j):
        at = pl.ds(pl.multiple_of(j * CHUNK, CHUNK), CHUNK)
        slot = lax.rem(j, d_slots)
        return pltpu.make_async_copy(down_ref.at[at, :], dbuf.at[slot], dsem.at[slot])

    def each(lo, hi, body):
        def step(i, carry):
            body(i)
            return carry
        lax.fori_loop(lo, hi, step, 0)

    barrier = pltpu.get_barrier_semaphore()

    def greet(row, col):
        pl.semaphore_signal(barrier, inc=1, device_id=(row, col), device_id_type=MESH)

    greet(r, sib)
    each(1, chips, lambda k: greet(r, peer(k) * 2 + core))
    greet(inner, c)

    @pl.when(jnp.logical_not(end))
    def _():
        greet(outer, c)

    early = min(6, u_slots)
    each(0, early, lambda j: load_up(j).start())

    mine = tok_ref[...].astype(jnp.float32)
    own[...] = jnp.zeros_like(own)
    for q in range(SPLIT):
        own[q * tok:(q + 1) * tok, :] = mine[:, q * wide:(q + 1) * wide]
    gath[c] = own[...].astype(jnp.bfloat16)

    @pl.when(end)
    def _():
        pl.semaphore_wait(barrier, chips + 1)

    @pl.when(jnp.logical_not(end))
    def _():
        pl.semaphore_wait(barrier, chips + 2)

    def gather_copy(src, send, col):
        return pltpu.make_async_remote_copy(
            src_ref=gath.at[src], dst_ref=gath.at[src], send_sem=send, recv_sem=g_recv.at[src],
            device_id=(r, col), device_id_type=MESH)

    each(1, chips, lambda k: gather_copy(c, g_send.at[k], peer(k) * 2 + core).start())
    gather_copy(c, g_send.at[0], sib).start()
    each(early, u_slots, lambda j: load_up(j).start())

    def forward(k):
        src = peer(k) * 2 + core
        gather_copy(src, f_send.at[k], sib).wait_recv()
        gather_copy(src, f_send.at[k], sib).start()

    each(1, chips, forward)
    each(0, d_slots, lambda j: load_down(j).start())
    each(0, chips, lambda k: gather_copy(peer(k) * 2 + 1 - core, g_send.at[0], sib).wait_recv())
    each(1, chips, lambda k: gather_copy(c, g_send.at[k], sib).wait_send())
    gather_copy(c, g_send.at[0], sib).wait_send()
    each(1, chips, lambda k: gather_copy(peer(k) * 2 + core, f_send.at[k], sib).wait_send())

    for d in range(cols):
        slab = gath[d].astype(jnp.float32)
        for q in range(SPLIT):
            acc[d * tok:(d + 1) * tok, q * wide:(q + 1) * wide] = slab[q * tok:(q + 1) * tok, :]
    xg[...] = acc[...].astype(jnp.bfloat16)
    acc[...] = jnp.zeros_like(acc)

    def inward(j, dst, sem):
        return pltpu.make_async_remote_copy(
            src_ref=sbuf.at[j], dst_ref=dst.at[j], send_sem=in_send.at[j], recv_sem=sem.at[j],
            device_id=(inner, c), device_id_type=MESH)

    def outward(j):
        return pltpu.make_async_remote_copy(
            src_ref=act.at[j], dst_ref=rc.at[j], send_sem=out_send.at[j], recv_sem=c_recv.at[j],
            device_id=(outer, c), device_id_type=MESH)

    lag_in = 1 + 4 * (half - 1 - depth)
    lag_out = 4 * half + 6 * depth
    ticks = n + 4 * half + 6 * (half - 1)

    def tick(t):
        a = t - lag_in

        @pl.when((a >= 0) & (a < n))
        def _():
            @pl.when(jnp.logical_not(end))
            def _():
                inward(a, rin, in_recv).wait_recv()
                part[a] = part[a] + rin[a].astype(jnp.float32)

            sbuf[a] = part[a].astype(jnp.bfloat16)

            @pl.when(centre)
            def _():
                inward(a, rc, c_recv).start()

            @pl.when(jnp.logical_not(centre))
            def _():
                inward(a, rin, in_recv).start()

        b = t - lag_out

        @pl.when((b >= 0) & (b < n))
        def _():
            outward(b).wait_recv()

            @pl.when(centre)
            def _():
                bias = ub_ref[:, pl.ds(pl.multiple_of(b * CHUNK, CHUNK), CHUNK)]
                act[b] = gelu(part[b] + rc[b].astype(jnp.float32) + bias).astype(jnp.bfloat16)

            @pl.when(jnp.logical_not(centre))
            def _():
                act[b] = rc[b]

            @pl.when(jnp.logical_not(end))
            def _():
                outward(b).start()

        @pl.when(t < n)
        def _():
            load_up(t).wait()
            part[t] = jnp.dot(xg[...], ubuf[lax.rem(t, u_slots)], preferred_element_type=jnp.float32)

            @pl.when(t + u_slots < n)
            def _():
                load_up(t + u_slots).start()

        @pl.when((b >= 0) & (b < n))
        def _():
            load_down(b).wait()
            acc[...] += jnp.dot(act[b], dbuf[lax.rem(b, d_slots)], preferred_element_type=jnp.float32)

            @pl.when(b + d_slots < n)
            def _():
                load_down(b + d_slots).start()

    each(0, ticks, tick)

    if packf.shape[1] != SPLIT * tok:
        packf[...] = jnp.zeros_like(packf)
    for d in range(cols):
        for q in range(SPLIT):
            packf[d, q * tok:(q + 1) * tok, :] = acc[d * tok:(d + 1) * tok, q * wide:(q + 1) * wide]

    def to_sibling(k):
        return pltpu.make_async_remote_copy(
            src_ref=sib_out.at[k], dst_ref=sib_in.at[k], send_sem=s1_send.at[k], recv_sem=s1_recv.at[k],
            device_id=(r, sib), device_id_type=MESH)

    def to_peer(k):
        return pltpu.make_async_remote_copy(
            src_ref=peer_out.at[k], dst_ref=peer_in.at[k], send_sem=s2_send.at[k], recv_sem=s2_recv.at[k],
            device_id=(r, peer(k) * 2 + core), device_id_type=MESH)

    def first(i):
        k = lax.rem(i, chips)
        sib_out[k] = packf[peer(k) * 2 + 1 - core].astype(jnp.bfloat16)
        to_sibling(k).start()

    def second(k):
        to_sibling(k).wait_recv()
        peer_out[k] = (packf[peer(k) * 2 + core] + sib_in[k].astype(jnp.float32)).astype(jnp.bfloat16)
        to_peer(k).start()

    each(1, chips + 1, first)
    each(1, chips, second)
    to_sibling(0).wait_recv()
    own[...] = packf[c] + sib_in[0].astype(jnp.float32)

    def third(k):
        to_peer(k).wait_recv()
        own[...] += peer_in[k].astype(jnp.float32)

    each(1, chips, third)
    for q in range(SPLIT):
        at = slice(q * wide, (q + 1) * wide)
        out_ref[:, at] = (
            tok_ref[:, at].astype(jnp.float32) + own[q * tok:(q + 1) * tok, :] + db_ref[:, at]
        ).astype(out_ref.dtype)

    each(0, chips, lambda k: to_sibling(k).wait_send())
    each(1, chips, lambda k: to_peer(k).wait_send())
    each(0, n, lambda j: inward(j, rin, in_recv).wait_send())

    @pl.when(jnp.logical_not(end))
    def _():
        each(0, n, lambda j: outward(j).wait_send())


def on_device(rows, cols, tokens, up_weight, up_bias, down_weight, down_bias):
    tok, feat = tokens.shape
    hidden = up_weight.shape[1]
    n = hidden // CHUNK
    m = tok * cols
    chips = cols // 2
    chunk_bytes = feat * CHUNK * 2
    u_slots = max(1, min(n, 28 * 1024 * 1024 // chunk_bytes))
    d_slots = max(1, min(n, 18 * 1024 * 1024 // chunk_bytes))
    tall = -(-tok * SPLIT // 16) * 16
    wide = feat // SPLIT
    bf16, f32 = jnp.bfloat16, jnp.float32
    vmem, dma = pltpu.VMEM, pltpu.SemaphoreType.DMA
    in_vmem = pl.BlockSpec(memory_space=pltpu.VMEM)
    in_place = pl.BlockSpec(memory_space=pl.ANY)
    return pl.pallas_call(
        functools.partial(kernel, rows, cols),
        out_shape=jax.ShapeDtypeStruct((tok, feat), bf16),
        in_specs=[in_vmem, in_place, in_vmem, in_place, in_vmem],
        out_specs=in_vmem,
        scratch_shapes=[
            vmem((u_slots, feat, CHUNK), bf16),
            vmem((d_slots, CHUNK, feat), bf16),
            vmem((cols, tall, wide), bf16),
            vmem((m, feat), bf16),
            vmem((n, m, CHUNK), f32),
            vmem((n, m, CHUNK), bf16),
            vmem((n, m, CHUNK), bf16),
            vmem((n, m, CHUNK), bf16),
            vmem((n, m, CHUNK), bf16),
            vmem((m, feat), f32),
            vmem((cols, tall, wide), f32),
            vmem((tall, wide), f32),
            vmem((chips, tall, wide), bf16),
            vmem((chips, tall, wide), bf16),
            vmem((chips, tall, wide), bf16),
            vmem((chips, tall, wide), bf16),
            dma((u_slots,)),
            dma((d_slots,)),
            dma((chips,)),
            dma((cols,)),
            dma((chips,)),
            dma((n,)),
            dma((n,)),
            dma((n,)),
            dma((n,)),
            dma((chips,)),
            dma((chips,)),
            dma((chips,)),
            dma((chips,)),
        ],
        cost_estimate=pl.CostEstimate(
            flops=4 * m * feat * hidden, bytes_accessed=4 * feat * hidden, transcendentals=m * hidden),
        compiler_params=pltpu.CompilerParams(
            collective_id=0, has_side_effects=True, vmem_limit_bytes=63 * 1024 * 1024),
    )(tokens, up_weight, up_bias.reshape(1, -1), down_weight, down_bias.reshape(1, -1))


def solution(mesh):
    placed = (P("col", "row"), P("row", "col"), P("col"), P("col", "row"), P("row"))
    body = functools.partial(on_device, mesh.shape["row"], mesh.shape["col"])
    return jax.shard_map(body, mesh=mesh, in_specs=placed, out_specs=P("col", "row"), check_vma=False)
```

```python
import functools

import jax
import jax.numpy as jnp
from jax import lax
from jax.experimental import pallas as pl
from jax.experimental.pallas import tpu as pltpu
from jax.sharding import PartitionSpec as P

CHUNK = 256
SPLIT = 4
MESH = pl.DeviceIdType.MESH


def gelu(v):
    return 0.5 * v * (1.0 + jnp.tanh(0.7978845608028654 * (v + 0.044715 * (v * v * v))))


def kernel(
    rows, cols, tok_ref, up_ref, ub_ref, down_ref, db_ref, out_ref,
    ubuf, dbuf, gath, xg, part, sbuf, rin, rc, act, acc, own, packf, sib_out, sib_in, peer_out, peer_in,
    usem, dsem, g_send, g_recv, f_send, in_send, in_recv, out_send, c_recv,
    s1_send, s1_recv, s2_send, s2_recv,
):
    tok, feat = tok_ref.shape
    wide = feat // SPLIT
    n = up_ref.shape[1] // CHUNK
    u_slots, d_slots = ubuf.shape[0], dbuf.shape[0]
    chips = cols // 2
    near = chips * tok
    halves, _, span = sib_out.shape
    narrow = span // SPLIT
    half = rows // 2
    r, c = lax.axis_index("row"), lax.axis_index("col")
    chip, core = c // 2, lax.rem(c, 2)
    sib = chip * 2 + 1 - core
    low = r < half
    depth = jnp.where(low, half - 1 - r, r - half)
    inner = jnp.where(low, r + 1, r - 1)
    outer = jnp.where(low, r - 1, r + 1)
    centre, end = depth == 0, depth == half - 1

    def peer(k):
        return lax.rem(chip + k, chips)

    def load_up(j):
        at = pl.ds(pl.multiple_of(j * CHUNK, CHUNK), CHUNK)
        slot = lax.rem(j, u_slots)
        return pltpu.make_async_copy(up_ref.at[:, at], ubuf.at[slot], usem.at[slot])

    def load_down(j):
        at = pl.ds(pl.multiple_of(j * CHUNK, CHUNK), CHUNK)
        slot = lax.rem(j, d_slots)
        return pltpu.make_async_copy(down_ref.at[at, :], dbuf.at[slot], dsem.at[slot])

    def each(lo, hi, body):
        def step(i, carry):
            body(i)
            return carry
        lax.fori_loop(lo, hi, step, 0)

    barrier = pltpu.get_barrier_semaphore()

    def greet(row, col):
        pl.semaphore_signal(barrier, inc=1, device_id=(row, col), device_id_type=MESH)

    greet(r, sib)
    each(1, chips, lambda k: greet(r, peer(k) * 2 + core))
    greet(inner, c)

    @pl.when(jnp.logical_not(end))
    def _():
        greet(outer, c)

    early = min(6, u_slots)
    each(0, early, lambda j: load_up(j).start())

    mine = tok_ref[...].astype(jnp.float32)
    own[...] = jnp.zeros_like(own)
    packf[...] = jnp.zeros_like(packf)
    for q in range(SPLIT):
        own[q * tok:(q + 1) * tok, :] = mine[:, q * wide:(q + 1) * wide]
    gath[0] = own[...].astype(jnp.bfloat16)

    @pl.when(end)
    def _():
        pl.semaphore_wait(barrier, chips + 1)

    @pl.when(jnp.logical_not(end))
    def _():
        pl.semaphore_wait(barrier, chips + 2)

    def gather_copy(k):
        return pltpu.make_async_remote_copy(
            src_ref=gath.at[0], dst_ref=gath.at[chips - k], send_sem=g_send.at[k], recv_sem=g_recv.at[chips - k],
            device_id=(r, peer(k) * 2 + core), device_id_type=MESH)

    swap = pltpu.make_async_remote_copy(
        src_ref=xg.at[pl.ds(0, near)], dst_ref=xg.at[pl.ds(near, near)], send_sem=f_send.at[0], recv_sem=f_send.at[1],
        device_id=(r, sib), device_id_type=MESH)

    each(1, chips, lambda k: gather_copy(k).start())
    each(early, u_slots, lambda j: load_up(j).start())
    for k in range(chips):
        if k > 0:
            gather_copy(chips - k).wait_recv()
        slab = gath[k].astype(jnp.float32)
        for q in range(SPLIT):
            acc[k * tok:(k + 1) * tok, q * wide:(q + 1) * wide] = slab[q * tok:(q + 1) * tok, :]
    xg[0:near] = acc[0:near].astype(jnp.bfloat16)
    swap.start()
    each(0, d_slots, lambda j: load_down(j).start())
    acc[...] = jnp.zeros_like(acc)
    each(1, chips, lambda k: gather_copy(k).wait_send())
    swap.wait()

    def inward(j, dst, sem):
        return pltpu.make_async_remote_copy(
            src_ref=sbuf.at[j], dst_ref=dst.at[j], send_sem=in_send.at[j], recv_sem=sem.at[j],
            device_id=(inner, c), device_id_type=MESH)

    def outward(j):
        return pltpu.make_async_remote_copy(
            src_ref=act.at[j], dst_ref=rc.at[j], send_sem=out_send.at[j], recv_sem=c_recv.at[j],
            device_id=(outer, c), device_id_type=MESH)

    lag_in = 1 + 4 * (half - 1 - depth)
    lag_out = 4 * half + 6 * depth
    ticks = n + 4 * half + 6 * (half - 1)

    def tick(t):
        a = t - lag_in

        @pl.when((a >= 0) & (a < n))
        def _():
            @pl.when(jnp.logical_not(end))
            def _():
                inward(a, rin, in_recv).wait_recv()
                part[a] = part[a] + rin[a].astype(jnp.float32)

            sbuf[a] = part[a].astype(jnp.bfloat16)

            @pl.when(centre)
            def _():
                inward(a, rc, c_recv).start()

            @pl.when(jnp.logical_not(centre))
            def _():
                inward(a, rin, in_recv).start()

        b = t - lag_out

        @pl.when((b >= 0) & (b < n))
        def _():
            outward(b).wait_recv()

            @pl.when(centre)
            def _():
                bias = ub_ref[:, pl.ds(pl.multiple_of(b * CHUNK, CHUNK), CHUNK)]
                act[b] = gelu(part[b] + rc[b].astype(jnp.float32) + bias).astype(jnp.bfloat16)

            @pl.when(jnp.logical_not(centre))
            def _():
                act[b] = rc[b]

            @pl.when(jnp.logical_not(end))
            def _():
                outward(b).start()

        @pl.when(t < n)
        def _():
            load_up(t).wait()
            part[t] = jnp.dot(xg[...], ubuf[lax.rem(t, u_slots)], preferred_element_type=jnp.float32)

            @pl.when(t + u_slots < n)
            def _():
                load_up(t + u_slots).start()

        @pl.when((b >= 0) & (b < n))
        def _():
            load_down(b).wait()
            acc[...] += jnp.dot(act[b], dbuf[lax.rem(b, d_slots)], preferred_element_type=jnp.float32)

            @pl.when(b + d_slots < n)
            def _():
                load_down(b + d_slots).start()

    each(0, ticks, tick)

    def to_sibling(h):
        return pltpu.make_async_remote_copy(
            src_ref=sib_out.at[h], dst_ref=sib_in.at[h], send_sem=s1_send.at[h], recv_sem=s1_recv.at[h],
            device_id=(r, sib), device_id_type=MESH)

    def to_peer(h, k):
        there = h * chips + chips - k
        return pltpu.make_async_remote_copy(
            src_ref=peer_out.at[h * chips + k], dst_ref=peer_in.at[there],
            send_sem=s2_send.at[h * chips + k], recv_sem=s2_recv.at[there],
            device_id=(r, peer(k) * 2 + core), device_id_type=MESH)

    for h in range(halves):
        sib_out[h] = acc[near:2 * near, h * span:(h + 1) * span].astype(jnp.bfloat16)
        to_sibling(h).start()
    for h in range(halves):
        at = slice(h * span, (h + 1) * span)
        to_sibling(h).wait_recv()
        acc[0:near, at] = acc[0:near, at] + sib_in[h].astype(jnp.float32)
        for k in range(1, chips):
            for q in range(SPLIT):
                lo = h * span + q * narrow
                packf[q * tok:(q + 1) * tok, :] = acc[k * tok:(k + 1) * tok, lo:lo + narrow]
            peer_out[h * chips + k] = packf[...].astype(jnp.bfloat16)
            to_peer(h, k).start()
    for h in range(halves):
        at = slice(h * span, (h + 1) * span)
        acc[0:tok, at] = acc[0:tok, at] + (tok_ref[:, at].astype(jnp.float32) + db_ref[:, at])
        for k in range(1, chips):
            to_peer(h, chips - k).wait_recv()
            slab = peer_in[h * chips + k].astype(jnp.float32)
            for q in range(SPLIT):
                lo = h * span + q * narrow
                acc[0:tok, lo:lo + narrow] = acc[0:tok, lo:lo + narrow] + slab[q * tok:(q + 1) * tok, :]
        out_ref[:, at] = acc[0:tok, at].astype(out_ref.dtype)

    for h in range(halves):
        to_sibling(h).wait_send()
        each(1, chips, lambda k, h=h: to_peer(h, k).wait_send())
    each(0, n, lambda j: inward(j, rin, in_recv).wait_send())

    @pl.when(jnp.logical_not(end))
    def _():
        each(0, n, lambda j: outward(j).wait_send())


def on_device(rows, cols, tokens, up_weight, up_bias, down_weight, down_bias):
    tok, feat = tokens.shape
    hidden = up_weight.shape[1]
    n = hidden // CHUNK
    m = tok * cols
    chips = cols // 2
    chunk_bytes = feat * CHUNK * 2
    u_slots = max(1, min(n, 28 * 1024 * 1024 // chunk_bytes))
    d_slots = max(1, min(n, 18 * 1024 * 1024 // chunk_bytes))
    tall = -(-tok * SPLIT // 16) * 16
    wide = feat // SPLIT
    halves = 2 if feat % (2 * SPLIT * 128) == 0 else 1
    span = feat // halves
    bf16, f32 = jnp.bfloat16, jnp.float32
    vmem, dma = pltpu.VMEM, pltpu.SemaphoreType.DMA
    in_vmem = pl.BlockSpec(memory_space=pltpu.VMEM)
    in_place = pl.BlockSpec(memory_space=pl.ANY)
    return pl.pallas_call(
        functools.partial(kernel, rows, cols),
        out_shape=jax.ShapeDtypeStruct((tok, feat), bf16),
        in_specs=[in_vmem, in_place, in_vmem, in_place, in_vmem],
        out_specs=in_vmem,
        scratch_shapes=[
            vmem((u_slots, feat, CHUNK), bf16),
            vmem((d_slots, CHUNK, feat), bf16),
            vmem((chips, tall, wide), bf16),
            vmem((m, feat), bf16),
            vmem((n, m, CHUNK), f32),
            vmem((n, m, CHUNK), bf16),
            vmem((n, m, CHUNK), bf16),
            vmem((n, m, CHUNK), bf16),
            vmem((n, m, CHUNK), bf16),
            vmem((m, feat), f32),
            vmem((tall, wide), f32),
            vmem((tall, span // SPLIT), f32),
            vmem((halves, m // 2, span), bf16),
            vmem((halves, m // 2, span), bf16),
            vmem((halves * chips, tall, span // SPLIT), bf16),
            vmem((halves * chips, tall, span // SPLIT), bf16),
            dma((u_slots,)),
            dma((d_slots,)),
            dma((chips,)),
            dma((chips,)),
            dma((2,)),
            dma((n,)),
            dma((n,)),
            dma((n,)),
            dma((n,)),
            dma((halves,)),
            dma((halves,)),
            dma((halves * chips,)),
            dma((halves * chips,)),
        ],
        cost_estimate=pl.CostEstimate(
            flops=4 * m * feat * hidden, bytes_accessed=4 * feat * hidden, transcendentals=m * hidden),
        compiler_params=pltpu.CompilerParams(
            collective_id=0, has_side_effects=True, vmem_limit_bytes=63 * 1024 * 1024),
    )(tokens, up_weight, up_bias.reshape(1, -1), down_weight, down_bias.reshape(1, -1))


def solution(mesh):
    placed = (P("col", "row"), P("row", "col"), P("col"), P("col", "row"), P("row"))
    body = functools.partial(on_device, mesh.shape["row"], mesh.shape["col"])
    return jax.shard_map(body, mesh=mesh, in_specs=placed, out_specs=P("col", "row"), check_vma=False)
```

```python
import functools

import jax
import jax.numpy as jnp
from jax import lax
from jax.experimental import pallas as pl
from jax.experimental.pallas import tpu as pltpu
from jax.sharding import PartitionSpec as P

PIECE = 256
SPLIT = 4
MESH = pl.DeviceIdType.MESH


def gelu(v):
    return 0.5 * v * (1.0 + jnp.tanh(0.7978845608028654 * (v + 0.044715 * (v * v * v))))


def kernel(
    rows, cols, tok_ref, up_ref, ub_ref, down_ref, db_ref, out_ref,
    ubuf, dbuf, gath, xg, part, sbuf, rin, rc, act, acc, own, packf, sib_out, sib_in, peer_out, peer_in,
    usem, dsem, g_send, g_recv, f_send, in_send, in_recv, out_send, c_recv,
    s1_send, s1_recv, s2_send, s2_recv,
):
    tok, feat = tok_ref.shape
    wide = feat // SPLIT
    chunk = ubuf.shape[2]
    n = up_ref.shape[1] // chunk
    pieces = chunk // PIECE
    u_slots, d_slots = ubuf.shape[0], dbuf.shape[0]
    chips = cols // 2
    near = chips * tok
    halves, _, span = sib_out.shape
    narrow = span // SPLIT
    half = rows // 2
    r, c = lax.axis_index("row"), lax.axis_index("col")
    chip, core = c // 2, lax.rem(c, 2)
    sib = chip * 2 + 1 - core
    low = r < half
    depth = jnp.where(low, half - 1 - r, r - half)
    inner = jnp.where(low, r + 1, r - 1)
    outer = jnp.where(low, r - 1, r + 1)
    centre, end = depth == 0, depth == half - 1

    def peer(k):
        return lax.rem(chip + k, chips)

    def load_up(j):
        at = pl.ds(pl.multiple_of(j * chunk, chunk), chunk)
        slot = lax.rem(j, u_slots)
        return pltpu.make_async_copy(up_ref.at[:, at], ubuf.at[slot], usem.at[slot])

    def load_down(j):
        at = pl.ds(pl.multiple_of(j * chunk, chunk), chunk)
        slot = lax.rem(j, d_slots)
        return pltpu.make_async_copy(down_ref.at[at, :], dbuf.at[slot], dsem.at[slot])

    def each(lo, hi, body):
        def step(i, carry):
            body(i)
            return carry
        lax.fori_loop(lo, hi, step, 0)

    barrier = pltpu.get_barrier_semaphore()

    def greet(row, col):
        pl.semaphore_signal(barrier, inc=1, device_id=(row, col), device_id_type=MESH)

    greet(r, sib)
    each(1, chips, lambda k: greet(r, peer(k) * 2 + core))
    greet(inner, c)

    @pl.when(jnp.logical_not(end))
    def _():
        greet(outer, c)

    early = min(3, u_slots)
    each(0, early, lambda j: load_up(j).start())

    mine = tok_ref[...].astype(jnp.float32)
    own[...] = jnp.zeros_like(own)
    packf[...] = jnp.zeros_like(packf)
    for q in range(SPLIT):
        own[q * tok:(q + 1) * tok, :] = mine[:, q * wide:(q + 1) * wide]
    gath[0] = own[...].astype(jnp.bfloat16)

    @pl.when(end)
    def _():
        pl.semaphore_wait(barrier, chips + 1)

    @pl.when(jnp.logical_not(end))
    def _():
        pl.semaphore_wait(barrier, chips + 2)

    def gather_copy(k):
        return pltpu.make_async_remote_copy(
            src_ref=gath.at[0], dst_ref=gath.at[chips - k], send_sem=g_send.at[k], recv_sem=g_recv.at[chips - k],
            device_id=(r, peer(k) * 2 + core), device_id_type=MESH)

    swap = pltpu.make_async_remote_copy(
        src_ref=xg.at[pl.ds(0, near)], dst_ref=xg.at[pl.ds(near, near)], send_sem=f_send.at[0], recv_sem=f_send.at[1],
        device_id=(r, sib), device_id_type=MESH)

    each(1, chips, lambda k: gather_copy(k).start())
    each(early, u_slots, lambda j: load_up(j).start())
    for k in range(chips):
        if k > 0:
            gather_copy(chips - k).wait_recv()
        slab = gath[k].astype(jnp.float32)
        for q in range(SPLIT):
            acc[k * tok:(k + 1) * tok, q * wide:(q + 1) * wide] = slab[q * tok:(q + 1) * tok, :]
    xg[0:near] = acc[0:near].astype(jnp.bfloat16)
    swap.start()
    each(0, d_slots, lambda j: load_down(j).start())
    acc[...] = jnp.zeros_like(acc)
    each(1, chips, lambda k: gather_copy(k).wait_send())
    swap.wait()

    def inward(j, dst, sem):
        return pltpu.make_async_remote_copy(
            src_ref=sbuf.at[j], dst_ref=dst.at[j], send_sem=in_send.at[j], recv_sem=sem.at[j],
            device_id=(inner, c), device_id_type=MESH)

    def outward(j, p):
        i = j * pieces + p
        return pltpu.make_async_remote_copy(
            src_ref=act.at[j, :, pl.ds(p * PIECE, PIECE)], dst_ref=rc.at[i],
            send_sem=out_send.at[i], recv_sem=c_recv.at[i],
            device_id=(outer, c), device_id_type=MESH)

    lag_in = 1 + 2 * (half - 1 - depth)
    lag_out = 2 * half + 1 + 3 * depth
    ticks = n + 2 * half + 1 + 3 * (half - 1)

    def tick(t):
        a = t - lag_in

        @pl.when((a >= 0) & (a < n))
        def _():
            for p in range(pieces):
                i = a * pieces + p
                at = slice(p * PIECE, (p + 1) * PIECE)

                @pl.when(jnp.logical_not(end))
                def _():
                    inward(i, rin, in_recv).wait_recv()
                    part[a, :, at] = part[a, :, at] + rin[i].astype(jnp.float32)

                sbuf[i] = part[a, :, at].astype(jnp.bfloat16)

                @pl.when(centre)
                def _():
                    inward(i, rc, c_recv).start()

                @pl.when(jnp.logical_not(centre))
                def _():
                    inward(i, rin, in_recv).start()

        b = t - lag_out

        @pl.when((b >= 0) & (b < n))
        def _():
            for p in range(pieces):
                i = b * pieces + p
                at = slice(p * PIECE, (p + 1) * PIECE)
                outward(b, p).wait_recv()

                @pl.when(centre)
                def _():
                    bias = ub_ref[:, pl.ds(pl.multiple_of(i * PIECE, PIECE), PIECE)]
                    total = part[b, :, at] + rc[i].astype(jnp.float32)
                    act[b, :, at] = gelu(total + bias).astype(jnp.bfloat16)

                @pl.when(jnp.logical_not(centre))
                def _():
                    act[b, :, at] = rc[i]

                @pl.when(jnp.logical_not(end))
                def _():
                    outward(b, p).start()

        @pl.when(t < n)
        def _():
            load_up(t).wait()
            part[t] = jnp.dot(xg[...], ubuf[lax.rem(t, u_slots)], preferred_element_type=jnp.float32)

            @pl.when(t + u_slots < n)
            def _():
                load_up(t + u_slots).start()

        @pl.when((b >= 0) & (b < n))
        def _():
            load_down(b).wait()
            acc[...] += jnp.dot(act[b], dbuf[lax.rem(b, d_slots)], preferred_element_type=jnp.float32)

            @pl.when(b + d_slots < n)
            def _():
                load_down(b + d_slots).start()

    each(0, ticks, tick)

    def to_sibling(h):
        return pltpu.make_async_remote_copy(
            src_ref=sib_out.at[h], dst_ref=sib_in.at[h], send_sem=s1_send.at[h], recv_sem=s1_recv.at[h],
            device_id=(r, sib), device_id_type=MESH)

    def to_peer(h, k):
        there = h * chips + chips - k
        return pltpu.make_async_remote_copy(
            src_ref=peer_out.at[h * chips + k], dst_ref=peer_in.at[there],
            send_sem=s2_send.at[h * chips + k], recv_sem=s2_recv.at[there],
            device_id=(r, peer(k) * 2 + core), device_id_type=MESH)

    for h in range(halves):
        sib_out[h] = acc[near:2 * near, h * span:(h + 1) * span].astype(jnp.bfloat16)
        to_sibling(h).start()
    for h in range(halves):
        at = slice(h * span, (h + 1) * span)
        to_sibling(h).wait_recv()
        acc[0:near, at] = acc[0:near, at] + sib_in[h].astype(jnp.float32)
        for k in range(1, chips):
            for q in range(SPLIT):
                lo = h * span + q * narrow
                packf[q * tok:(q + 1) * tok, :] = acc[k * tok:(k + 1) * tok, lo:lo + narrow]
            peer_out[h * chips + k] = packf[...].astype(jnp.bfloat16)
            to_peer(h, k).start()
    for h in range(halves):
        at = slice(h * span, (h + 1) * span)
        acc[0:tok, at] = acc[0:tok, at] + (tok_ref[:, at].astype(jnp.float32) + db_ref[:, at])
        for k in range(1, chips):
            to_peer(h, chips - k).wait_recv()
            slab = peer_in[h * chips + k].astype(jnp.float32)
            for q in range(SPLIT):
                lo = h * span + q * narrow
                acc[0:tok, lo:lo + narrow] = acc[0:tok, lo:lo + narrow] + slab[q * tok:(q + 1) * tok, :]
        out_ref[:, at] = acc[0:tok, at].astype(out_ref.dtype)

    for h in range(halves):
        to_sibling(h).wait_send()
        each(1, chips, lambda k, h=h: to_peer(h, k).wait_send())
    each(0, n * pieces, lambda j: inward(j, rin, in_recv).wait_send())

    @pl.when(jnp.logical_not(end))
    def _():
        for p in range(pieces):
            each(0, n, lambda j, p=p: outward(j, p).wait_send())


def on_device(rows, cols, tokens, up_weight, up_bias, down_weight, down_bias):
    tok, feat = tokens.shape
    hidden = up_weight.shape[1]
    chunk = 2 * PIECE if hidden % (2 * PIECE) == 0 else PIECE
    n, sent = hidden // chunk, hidden // PIECE
    m = tok * cols
    chips = cols // 2
    chunk_bytes = feat * chunk * 2
    u_slots = max(1, min(n, 28 * 1024 * 1024 // chunk_bytes))
    d_slots = max(1, min(n, 18 * 1024 * 1024 // chunk_bytes))
    tall = -(-tok * SPLIT // 16) * 16
    wide = feat // SPLIT
    halves = 2 if feat % (2 * SPLIT * 128) == 0 else 1
    span = feat // halves
    bf16, f32 = jnp.bfloat16, jnp.float32
    vmem, dma = pltpu.VMEM, pltpu.SemaphoreType.DMA
    in_vmem = pl.BlockSpec(memory_space=pltpu.VMEM)
    in_place = pl.BlockSpec(memory_space=pl.ANY)
    return pl.pallas_call(
        functools.partial(kernel, rows, cols),
        out_shape=jax.ShapeDtypeStruct((tok, feat), bf16),
        in_specs=[in_vmem, in_place, in_vmem, in_place, in_vmem],
        out_specs=in_vmem,
        scratch_shapes=[
            vmem((u_slots, feat, chunk), bf16),
            vmem((d_slots, chunk, feat), bf16),
            vmem((chips, tall, wide), bf16),
            vmem((m, feat), bf16),
            vmem((n, m, chunk), f32),
            vmem((sent, m, PIECE), bf16),
            vmem((sent, m, PIECE), bf16),
            vmem((sent, m, PIECE), bf16),
            vmem((n, m, chunk), bf16),
            vmem((m, feat), f32),
            vmem((tall, wide), f32),
            vmem((tall, span // SPLIT), f32),
            vmem((halves, m // 2, span), bf16),
            vmem((halves, m // 2, span), bf16),
            vmem((halves * chips, tall, span // SPLIT), bf16),
            vmem((halves * chips, tall, span // SPLIT), bf16),
            dma((u_slots,)),
            dma((d_slots,)),
            dma((chips,)),
            dma((chips,)),
            dma((2,)),
            dma((sent,)),
            dma((sent,)),
            dma((sent,)),
            dma((sent,)),
            dma((halves,)),
            dma((halves,)),
            dma((halves * chips,)),
            dma((halves * chips,)),
        ],
        cost_estimate=pl.CostEstimate(
            flops=4 * m * feat * hidden, bytes_accessed=4 * feat * hidden, transcendentals=m * hidden),
        compiler_params=pltpu.CompilerParams(
            collective_id=0, has_side_effects=True, vmem_limit_bytes=63 * 1024 * 1024),
    )(tokens, up_weight, up_bias.reshape(1, -1), down_weight, down_bias.reshape(1, -1))


def solution(mesh):
    placed = (P("col", "row"), P("row", "col"), P("col"), P("col", "row"), P("row"))
    body = functools.partial(on_device, mesh.shape["row"], mesh.shape["col"])
    return jax.shard_map(body, mesh=mesh, in_specs=placed, out_specs=P("col", "row"), check_vma=False)
```

```python
import functools

import jax
import jax.numpy as jnp
from jax import lax
from jax.experimental import pallas as pl
from jax.experimental.pallas import tpu as pltpu
from jax.sharding import PartitionSpec as P

PIECE = 128
SPLIT = 4
MESH = pl.DeviceIdType.MESH


def gelu(v):
    return 0.5 * v * (1.0 + jnp.tanh(0.7978845608028654 * (v + 0.044715 * (v * v * v))))


def kernel(
    rows, cols, tok_ref, up_ref, ub_ref, down_ref, db_ref, out_ref,
    ubuf, dbuf, gath, xg, part, sbuf, rin, rc, act, acc, own, packf, sib_out, sib_in, peer_out, peer_in,
    usem, dsem, g_send, g_recv, f_send, in_send, in_recv, out_send, c_recv,
    s1_send, s1_recv, s2_send, s2_recv,
):
    tok, feat = tok_ref.shape
    wide = feat // SPLIT
    chunk = ubuf.shape[2]
    n = up_ref.shape[1] // chunk
    pieces = chunk // PIECE
    u_slots, d_slots = ubuf.shape[0], dbuf.shape[0]
    chips = cols // 2
    near = chips * tok
    halves, _, span = sib_out.shape
    narrow = span // SPLIT
    half = rows // 2
    r, c = lax.axis_index("row"), lax.axis_index("col")
    chip, core = c // 2, lax.rem(c, 2)
    sib = chip * 2 + 1 - core
    low = r < half
    depth = jnp.where(low, half - 1 - r, r - half)
    inner = jnp.where(low, r + 1, r - 1)
    outer = jnp.where(low, r - 1, r + 1)
    centre, end = depth == 0, depth == half - 1

    def peer(k):
        return lax.rem(chip + k, chips)

    def load_up(j):
        at = pl.ds(pl.multiple_of(j * chunk, chunk), chunk)
        slot = lax.rem(j, u_slots)
        return pltpu.make_async_copy(up_ref.at[:, at], ubuf.at[slot], usem.at[slot])

    def load_down(j):
        at = pl.ds(pl.multiple_of(j * chunk, chunk), chunk)
        slot = lax.rem(j, d_slots)
        return pltpu.make_async_copy(down_ref.at[at, :], dbuf.at[slot], dsem.at[slot])

    def each(lo, hi, body):
        def step(i, carry):
            body(i)
            return carry
        lax.fori_loop(lo, hi, step, 0)

    barrier = pltpu.get_barrier_semaphore()

    def greet(row, col):
        pl.semaphore_signal(barrier, inc=1, device_id=(row, col), device_id_type=MESH)

    greet(r, sib)
    each(1, chips, lambda k: greet(r, peer(k) * 2 + core))
    greet(inner, c)

    @pl.when(jnp.logical_not(end))
    def _():
        greet(outer, c)

    early = min(6, u_slots)
    each(0, early, lambda j: load_up(j).start())

    mine = tok_ref[...].astype(jnp.float32)
    own[...] = jnp.zeros_like(own)
    packf[...] = jnp.zeros_like(packf)
    for q in range(SPLIT):
        own[q * tok:(q + 1) * tok, :] = mine[:, q * wide:(q + 1) * wide]
    gath[0] = own[...].astype(jnp.bfloat16)

    @pl.when(end)
    def _():
        pl.semaphore_wait(barrier, chips + 1)

    @pl.when(jnp.logical_not(end))
    def _():
        pl.semaphore_wait(barrier, chips + 2)

    def gather_copy(k):
        return pltpu.make_async_remote_copy(
            src_ref=gath.at[0], dst_ref=gath.at[chips - k], send_sem=g_send.at[k], recv_sem=g_recv.at[chips - k],
            device_id=(r, peer(k) * 2 + core), device_id_type=MESH)

    swap = pltpu.make_async_remote_copy(
        src_ref=xg.at[pl.ds(0, near)], dst_ref=xg.at[pl.ds(near, near)], send_sem=f_send.at[0], recv_sem=f_send.at[1],
        device_id=(r, sib), device_id_type=MESH)

    each(1, chips, lambda k: gather_copy(k).start())
    each(early, u_slots, lambda j: load_up(j).start())
    for k in range(chips):
        if k > 0:
            gather_copy(chips - k).wait_recv()
        slab = gath[k].astype(jnp.float32)
        for q in range(SPLIT):
            acc[k * tok:(k + 1) * tok, q * wide:(q + 1) * wide] = slab[q * tok:(q + 1) * tok, :]
    xg[0:near] = acc[0:near].astype(jnp.bfloat16)
    swap.start()
    each(0, d_slots, lambda j: load_down(j).start())
    acc[...] = jnp.zeros_like(acc)
    each(1, chips, lambda k: gather_copy(k).wait_send())
    swap.wait()

    def inward(j, dst, sem):
        return pltpu.make_async_remote_copy(
            src_ref=sbuf.at[j], dst_ref=dst.at[j], send_sem=in_send.at[j], recv_sem=sem.at[j],
            device_id=(inner, c), device_id_type=MESH)

    def outward(j, p):
        i = j * pieces + p
        return pltpu.make_async_remote_copy(
            src_ref=act.at[j, :, pl.ds(p * PIECE, PIECE)], dst_ref=rc.at[i],
            send_sem=out_send.at[i], recv_sem=c_recv.at[i],
            device_id=(outer, c), device_id_type=MESH)

    lag_in = 1 + 4 * (half - 1 - depth)
    lag_out = 4 * half + 6 * depth
    ticks = n + 4 * half + 6 * (half - 1)

    def tick(t):
        a = t - lag_in

        @pl.when((a >= 0) & (a < n))
        def _():
            for p in range(pieces):
                i = a * pieces + p
                at = slice(p * PIECE, (p + 1) * PIECE)

                @pl.when(jnp.logical_not(end))
                def _():
                    inward(i, rin, in_recv).wait_recv()
                    part[a, :, at] = part[a, :, at] + rin[i].astype(jnp.float32)

                sbuf[i] = part[a, :, at].astype(jnp.bfloat16)

                @pl.when(centre)
                def _():
                    inward(i, rc, c_recv).start()

                @pl.when(jnp.logical_not(centre))
                def _():
                    inward(i, rin, in_recv).start()

        b = t - lag_out

        @pl.when((b >= 0) & (b < n))
        def _():
            for p in range(pieces):
                i = b * pieces + p
                at = slice(p * PIECE, (p + 1) * PIECE)
                outward(b, p).wait_recv()

                @pl.when(centre)
                def _():
                    bias = ub_ref[:, pl.ds(pl.multiple_of(i * PIECE, PIECE), PIECE)]
                    total = part[b, :, at] + rc[i].astype(jnp.float32)
                    act[b, :, at] = gelu(total + bias).astype(jnp.bfloat16)

                @pl.when(jnp.logical_not(centre))
                def _():
                    act[b, :, at] = rc[i]

                @pl.when(jnp.logical_not(end))
                def _():
                    outward(b, p).start()

        @pl.when(t < n)
        def _():
            load_up(t).wait()
            part[t] = jnp.dot(xg[...], ubuf[lax.rem(t, u_slots)], preferred_element_type=jnp.float32)

            @pl.when(t + u_slots < n)
            def _():
                load_up(t + u_slots).start()

        @pl.when((b >= 0) & (b < n))
        def _():
            load_down(b).wait()
            acc[...] += jnp.dot(act[b], dbuf[lax.rem(b, d_slots)], preferred_element_type=jnp.float32)

            @pl.when(b + d_slots < n)
            def _():
                load_down(b + d_slots).start()

    each(0, ticks, tick)

    def to_sibling(h):
        return pltpu.make_async_remote_copy(
            src_ref=sib_out.at[h], dst_ref=sib_in.at[h], send_sem=s1_send.at[h], recv_sem=s1_recv.at[h],
            device_id=(r, sib), device_id_type=MESH)

    def to_peer(h, k):
        there = h * chips + chips - k
        return pltpu.make_async_remote_copy(
            src_ref=peer_out.at[h * chips + k], dst_ref=peer_in.at[there],
            send_sem=s2_send.at[h * chips + k], recv_sem=s2_recv.at[there],
            device_id=(r, peer(k) * 2 + core), device_id_type=MESH)

    for h in range(halves):
        sib_out[h] = acc[near:2 * near, h * span:(h + 1) * span].astype(jnp.bfloat16)
        to_sibling(h).start()
    for h in range(halves):
        at = slice(h * span, (h + 1) * span)
        to_sibling(h).wait_recv()
        acc[0:near, at] = acc[0:near, at] + sib_in[h].astype(jnp.float32)
        for k in range(1, chips):
            for q in range(SPLIT):
                lo = h * span + q * narrow
                packf[q * tok:(q + 1) * tok, :] = acc[k * tok:(k + 1) * tok, lo:lo + narrow]
            peer_out[h * chips + k] = packf[...].astype(jnp.bfloat16)
            to_peer(h, k).start()
    for h in range(halves):
        at = slice(h * span, (h + 1) * span)
        acc[0:tok, at] = acc[0:tok, at] + (tok_ref[:, at].astype(jnp.float32) + db_ref[:, at])
        for k in range(1, chips):
            to_peer(h, chips - k).wait_recv()
            slab = peer_in[h * chips + k].astype(jnp.float32)
            for q in range(SPLIT):
                lo = h * span + q * narrow
                acc[0:tok, lo:lo + narrow] = acc[0:tok, lo:lo + narrow] + slab[q * tok:(q + 1) * tok, :]
        out_ref[:, at] = acc[0:tok, at].astype(out_ref.dtype)

    for h in range(halves):
        to_sibling(h).wait_send()
        each(1, chips, lambda k, h=h: to_peer(h, k).wait_send())
    each(0, n * pieces, lambda j: inward(j, rin, in_recv).wait_send())

    @pl.when(jnp.logical_not(end))
    def _():
        for p in range(pieces):
            each(0, n, lambda j, p=p: outward(j, p).wait_send())


def on_device(rows, cols, tokens, up_weight, up_bias, down_weight, down_bias):
    tok, feat = tokens.shape
    hidden = up_weight.shape[1]
    chunk = 2 * PIECE if hidden % (2 * PIECE) == 0 else PIECE
    n, sent = hidden // chunk, hidden // PIECE
    m = tok * cols
    chips = cols // 2
    chunk_bytes = feat * chunk * 2
    u_slots = max(1, min(n, 28 * 1024 * 1024 // chunk_bytes))
    d_slots = max(1, min(n, 18 * 1024 * 1024 // chunk_bytes))
    tall = -(-tok * SPLIT // 16) * 16
    wide = feat // SPLIT
    halves = 2 if feat % (2 * SPLIT * 128) == 0 else 1
    span = feat // halves
    bf16, f32 = jnp.bfloat16, jnp.float32
    vmem, dma = pltpu.VMEM, pltpu.SemaphoreType.DMA
    in_vmem = pl.BlockSpec(memory_space=pltpu.VMEM)
    in_place = pl.BlockSpec(memory_space=pl.ANY)
    return pl.pallas_call(
        functools.partial(kernel, rows, cols),
        out_shape=jax.ShapeDtypeStruct((tok, feat), bf16),
        in_specs=[in_vmem, in_place, in_vmem, in_place, in_vmem],
        out_specs=in_vmem,
        scratch_shapes=[
            vmem((u_slots, feat, chunk), bf16),
            vmem((d_slots, chunk, feat), bf16),
            vmem((chips, tall, wide), bf16),
            vmem((m, feat), bf16),
            vmem((n, m, chunk), f32),
            vmem((sent, m, PIECE), bf16),
            vmem((sent, m, PIECE), bf16),
            vmem((sent, m, PIECE), bf16),
            vmem((n, m, chunk), bf16),
            vmem((m, feat), f32),
            vmem((tall, wide), f32),
            vmem((tall, span // SPLIT), f32),
            vmem((halves, m // 2, span), bf16),
            vmem((halves, m // 2, span), bf16),
            vmem((halves * chips, tall, span // SPLIT), bf16),
            vmem((halves * chips, tall, span // SPLIT), bf16),
            dma((u_slots,)),
            dma((d_slots,)),
            dma((chips,)),
            dma((chips,)),
            dma((2,)),
            dma((sent,)),
            dma((sent,)),
            dma((sent,)),
            dma((sent,)),
            dma((halves,)),
            dma((halves,)),
            dma((halves * chips,)),
            dma((halves * chips,)),
        ],
        cost_estimate=pl.CostEstimate(
            flops=4 * m * feat * hidden, bytes_accessed=4 * feat * hidden, transcendentals=m * hidden),
        compiler_params=pltpu.CompilerParams(
            collective_id=0, has_side_effects=True, vmem_limit_bytes=63 * 1024 * 1024),
    )(tokens, up_weight, up_bias.reshape(1, -1), down_weight, down_bias.reshape(1, -1))


def solution(mesh):
    placed = (P("col", "row"), P("row", "col"), P("col"), P("col", "row"), P("row"))
    body = functools.partial(on_device, mesh.shape["row"], mesh.shape["col"])
    return jax.shard_map(body, mesh=mesh, in_specs=placed, out_specs=P("col", "row"), check_vma=False)
```
